32 devices in a mesh: group: 2 (over y), row: 4 (over z), col: 4 (over x, core).
Axes of the slice: x: 2, y: 2, z: 4, core: 2. Of those that a mesh axis runs over, the one named last changes fastest.
Arguments:
- pair_repr: bfloat16 [256, 128, 128], P(('group', 'row'), 'col'), parts along dimension 0, may hold values from -6 to 6
- chain_ids: int32 [256], P('group'), parts along dimension 0, may hold values from 0 to 7, never falling along the last dimension, each value on 1 to 32 neighbouring positions
- valid_counts: int32 [16], P('group'), parts along dimension 0, may hold values from 8 to 32
- norm_gain: float32 [128], replicated, may hold values from 0.25 to 1.75
- norm_bias: float32 [128], replicated, may hold values from -3 to 3
- input_weights: bfloat16 [128, 384], replicated, may hold values from -0.5 to 0.5
- final_gain: float32 [64], replicated, may hold values from 0.25 to 1.75
- final_bias: float32 [64], replicated, may hold values from -3 to 3
- output_weight: bfloat16 [64, 128], replicated, may hold values from -0.75 to 0.75
- transition_in: bfloat16 [128, 1024], replicated, may hold values from -0.5 to 0.5
- transition_out: bfloat16 [512, 128], replicated, may hold values from -0.25 to 0.25
Outputs:
- update: bfloat16 [256, 128, 128], P(('group', 'row', 'col')), parts along dimension 0
The draws below stay inside these ranges and needn't reach their ends.
There are 2 independent parts, one for each index of `group`. The reference program is written for one: setup_inputs(seed, part) draws one part's arguments, and reference() takes and returns one part's arrays. A program takes and returns all parts, laid end to end along the dimension named above; an argument that names none is the same for every part. Nothing has to cross between parts.
Inputs may be any that keep to these rules, and one draw needn't show every extreme that they name: chain_ids never falls; each chain holds 1 to 32 tokens and one holds exactly 32.
All inputs are finite; a program needn't handle non-finite values.
Results may differ from the reference program's by a relative error of at most 0.0063.
Values may be sent and summed in bfloat16 or wider, within the bound.
A program may use at most 192 MiB of HBM per device.

```python
import math
import jax
import jax.numpy as jnp
import numpy as np
from jax import lax

C = 128
HC = 64
TRANS = 512
CHAINS = 8
N = 128


def touch_ends(result, rng, smallest, top_value):
    longest = result.shape.index(max(result.shape))
    spots = []
    for shift in (0, 1):
        where = [jax.random.randint(jax.random.fold_in(rng, axis), (), 0, length) for axis, length in enumerate(result.shape)]
        where[longest] = (where[longest] + shift) % result.shape[longest]
        spots.append(tuple(where))
    return result.at[spots[0]].set(smallest).at[spots[1]].set(top_value)


def level_of(rng, extent, cuts, low, largest):
    def one(axis_at, shards_of):
        draws = jax.random.uniform(jax.random.fold_in(jax.random.fold_in(rng, 6), axis_at), (shards_of,), jnp.float32, low / len(cuts), largest / len(cuts))
        return jnp.repeat(jnp.exp(draws), extent[axis_at] // shards_of).reshape((-1,) + (1,) * (len(extent) - axis_at - 1))

    level = one(*cuts[0])
    for cut in cuts[1:]:
        level = level * one(*cut)
    return level


def split_up(amount, total, most, slope):
    weights = [(1 << 20) // math.isqrt(rank ** slope) + 1 for rank in range(2, amount + 1)]
    surplus, holding = total - most - (amount - 1), [1] * (amount - 1)
    while surplus > 0:
        candidates = [i for i in range(amount - 1) if holding[i] < most]
        mass, left = sum([weights[i] for i in candidates]), surplus
        for i in candidates:
            extra = min(most - holding[i], max(1, left * weights[i] // mass), surplus)
            holding[i] = holding[i] + extra
            surplus = surplus - extra
    return np.array([most] + holding)


def ragged(stream_key, number_of, total, reach, slope):
    if number_of == 2:
        one = jax.random.randint(stream_key, (), max(1, total - reach), min(reach, total - 1) + 1)
        return jnp.stack([one, total - one])
    lengths = jnp.asarray(split_up(number_of, total, reach, slope), jnp.int32)
    pairs = (number_of - 1) // 2
    donor, sink = lengths[1:1 + 2 * pairs:2], lengths[2:2 + 2 * pairs:2]
    slack = jnp.minimum(donor - 1, reach - sink)
    shifted = jax.random.randint(jax.random.fold_in(stream_key, 1), (pairs,), 0, 1 << 20) % (slack + 1)
    lengths = lengths.at[1:1 + 2 * pairs:2].set(donor - shifted).at[2:2 + 2 * pairs:2].set(sink + shifted)
    return lengths[jax.random.permutation(jax.random.fold_in(stream_key, 2), number_of)]


def normal_values(stream_key, shape, width, reach, cuts=(), kind=jnp.bfloat16):
    entries = width * jax.random.normal(stream_key, shape, jnp.float32)
    if cuts:
        entries = entries * level_of(stream_key, shape, cuts, -0.22, 0.18)
    return jnp.clip(entries, -reach, reach).astype(kind)


def setup_inputs(seed: int = 0, part: int = 0) -> dict:
    key_list = jax.random.split(jax.random.key(seed), 12)
    part_keys = jax.random.split(jax.random.fold_in(key_list[11], part), 12)
    pair_repr = normal_values(part_keys[0], (N, N, C), 1.0, 6.0, ((0, 4), (1, 4)))
    chain_ids = jnp.searchsorted(jnp.cumsum(ragged(part_keys[1], CHAINS, N, N // 4, 1)), jnp.arange(N), side="right").astype(jnp.int32)
    valid_counts = touch_ends(jax.random.randint(part_keys[2], (CHAINS,), N // 16, N // 4 + 1), jax.random.fold_in(part_keys[2], 1), N // 16, (N // 4 + 1) - 1).astype(jnp.int32)
    norm_gain = jnp.clip(1.0 + 0.15 * jax.random.normal(key_list[3], (C,), jnp.float32), 0.25, 1.75)
    norm_bias = normal_values(key_list[4], (C,), 0.5, 3.0, (), jnp.float32)
    input_weights = normal_values(key_list[5], (C, 4 * HC + C), C ** -0.5, 0.5)
    final_gain = jnp.clip(1.0 + 0.15 * jax.random.normal(key_list[6], (HC,), jnp.float32), 0.25, 1.75)
    final_bias = normal_values(key_list[7], (HC,), 0.5, 3.0, (), jnp.float32)
    output_weight = normal_values(key_list[8], (HC, C), HC ** -0.5, 0.75)
    transition_in = normal_values(key_list[9], (C, 2 * TRANS), C ** -0.5, 0.5)
    transition_out = normal_values(key_list[10], (TRANS, C), TRANS ** -0.5, 0.25)
    return dict(pair_repr=pair_repr, chain_ids=chain_ids, valid_counts=valid_counts, norm_gain=norm_gain, norm_bias=norm_bias, input_weights=input_weights, final_gain=final_gain, final_bias=final_bias, output_weight=output_weight, transition_in=transition_in, transition_out=transition_out)


def token_valid_of(chain_ids, valid_counts):
    token_count = chain_ids.shape[0]
    labels = jnp.arange(valid_counts.shape[0], dtype=jnp.int32)
    before = (chain_ids[:, None] < labels[None, :]).astype(jnp.int32)
    starts = lax.optimization_barrier(jnp.sum(before, axis=0))
    member = (chain_ids[:, None] == labels[None, :]).astype(jnp.int32)
    first_index = lax.optimization_barrier(jnp.sum(member * starts[None, :], axis=1))
    limits = lax.optimization_barrier(jnp.sum(member * valid_counts[None, :], axis=1))
    position = jnp.arange(token_count, dtype=jnp.int32) - first_index
    return (position < limits).astype(jnp.float32)

def layer_norm(values, gain, bias):
    average = lax.optimization_barrier(jnp.mean(values, axis=-1, keepdims=True))
    centered = values - average
    spread = lax.optimization_barrier(jnp.mean(centered * centered, axis=-1, keepdims=True))
    return centered * lax.rsqrt(spread + 1e-05) * gain + bias

def reference(pair_repr, chain_ids, valid_counts, norm_gain, norm_bias, input_weights, final_gain, final_bias, output_weight, transition_in, transition_out):
    token_valid = token_valid_of(chain_ids, valid_counts)
    pair_valid = token_valid[:, None] * token_valid[None, :]
    normed = layer_norm(pair_repr.astype(jnp.float32), norm_gain, norm_bias).astype(jnp.bfloat16)
    projected = jnp.dot(normed.reshape(N * N, C), input_weights, preferred_element_type=jnp.float32).reshape(N, N, 4 * HC + C)
    left_side = (jax.nn.sigmoid(projected[..., HC:2 * HC]) * projected[..., :HC] * pair_valid[..., None]).astype(jnp.bfloat16)
    right_side = (jax.nn.sigmoid(projected[..., 3 * HC:4 * HC]) * projected[..., 2 * HC:3 * HC] * pair_valid[..., None]).astype(jnp.bfloat16)
    gate_value = jax.nn.sigmoid(projected[..., 4 * HC:])
    mixed_sum = jnp.einsum('ikc,jkc->ijc', left_side.astype(jnp.float32), right_side.astype(jnp.float32), precision=lax.Precision.HIGHEST)
    mixed_normed = layer_norm(mixed_sum, final_gain, final_bias).astype(jnp.bfloat16)
    outgoing = jnp.dot(mixed_normed.reshape(N * N, HC), output_weight, preferred_element_type=jnp.float32).reshape(N, N, C)

    def transition_row(normed_row):
        both = jnp.dot(normed_row, transition_in, preferred_element_type=jnp.float32)
        hidden_act = (jax.nn.silu(both[:, :TRANS]) * both[:, TRANS:]).astype(jnp.bfloat16)
        return jnp.dot(hidden_act, transition_out, preferred_element_type=jnp.float32)
    transition = lax.map(transition_row, normed)
    return (gate_value * outgoing + transition).astype(jnp.bfloat16)
```

```python
import functools

import jax
import jax.numpy as jnp
from jax import lax
from jax.experimental import pallas as pl
from jax.experimental.pallas import tpu as pltpu
from jax.sharding import PartitionSpec as P

MESH = pl.DeviceIdType.MESH
F32, BF16 = jnp.float32, jnp.bfloat16


def sigmoid(v):
    return 0.5 * jnp.tanh(0.5 * v) + 0.5


def column_of(row):
    n = row.shape[1]
    spot = lax.broadcasted_iota(jnp.int32, (n, n), 0) == lax.broadcasted_iota(jnp.int32, (n, n), 1)
    return jnp.sum(jnp.where(spot, row, 0.0), axis=1, keepdims=True)


def kernel(
    rows_n,
    cols_n,
    pair_ref,
    ids_ref,
    counts_ref,
    gain_ref,
    bias_ref,
    in_hbm,
    fgain_ref,
    fbias_ref,
    out_hbm,
    tin_hbm,
    tout_hbm,
    update_ref,
    x_ref,
    win_ref,
    wout_ref,
    tin_ref,
    tout_ref,
    normed_ref,
    lr_ref,
    rx_ref,
    tx_ref,
    mx_ref,
    gate_ref,
    trans_ref,
    local_sem,
    in_send,
    in_recv,
    a_send,
    a_recv,
    b_send,
    b_recv,
):
    peers = rows_n * cols_n
    own, tokens, channels = x_ref.shape
    width = pair_ref.shape[1]
    hidden = wout_ref.shape[0]
    trans = tout_ref.shape[0]
    share = hidden // peers
    row, col = lax.axis_index("row"), lax.axis_index("col")
    me = row * cols_n + col

    def at(offset):
        peer = lax.rem(me + offset, peers)
        return {"row": lax.div(peer, cols_n), "col": lax.rem(peer, cols_n)}, peer

    barrier = pltpu.get_barrier_semaphore()
    for o in range(1, peers):
        pl.semaphore_signal(barrier, inc=1, device_id=at(o)[0], device_id_type=MESH)
    locals_ = [
        pltpu.make_async_copy(
            pair_ref.at[pl.ds(col * own, own)],
            x_ref.at[:, pl.ds(col * width, width), :],
            local_sem.at[0],
        )
    ]
    for n, (a, b) in enumerate(
        ((in_hbm, win_ref), (out_hbm, wout_ref), (tin_hbm, tin_ref), (tout_hbm, tout_ref))
    ):
        locals_.append(pltpu.make_async_copy(a, b, local_sem.at[n + 1]))
    for c in locals_:
        c.start()
    pl.semaphore_wait(barrier, peers - 1)

    copies = []
    for o in range(1, cols_n):
        to = lax.rem(col + o, cols_n)
        copies.append(
            pltpu.make_async_remote_copy(
                src_ref=pair_ref.at[pl.ds(to * own, own)],
                dst_ref=x_ref.at[:, pl.ds(col * width, width), :],
                send_sem=in_send.at[o],
                recv_sem=in_recv.at[o],
                device_id={"row": row, "col": to},
                device_id_type=MESH,
            )
        )
    for c in copies:
        c.start()

    ids = ids_ref[...]
    first = jnp.zeros(ids.shape, F32)
    limit = jnp.zeros(ids.shape, jnp.int32)
    for label in range(counts_ref.shape[0]):
        start = jnp.sum(jnp.where(ids < label, 1.0, 0.0), axis=1, keepdims=True)
        first = jnp.where(ids == label, start, first)
        limit = jnp.where(ids == label, counts_ref[label], limit)
    spot = lax.broadcasted_iota(jnp.int32, ids.shape, 1).astype(F32)
    valid = jnp.where(spot - first < limit.astype(F32), 1.0, 0.0)
    wide = (own, tokens)
    mine = lax.broadcasted_iota(jnp.int32, wide, 1) == (
        me * own + lax.broadcasted_iota(jnp.int32, wide, 0)
    )
    valid_rows = jnp.sum(jnp.where(mine, valid, 0.0), axis=1, keepdims=True)
    pair_valid = valid_rows * valid
    fgain, fbias = column_of(fgain_ref[...]), column_of(fbias_ref[...])
    for c in locals_:
        c.wait()
    in_t = win_ref[:, : 4 * hidden].astype(F32).T.astype(BF16)
    for c in copies:
        c.wait()

    x = x_ref[...].reshape(own * tokens, channels).astype(F32)
    average = jnp.mean(x, axis=-1, keepdims=True)
    centered = x - average
    spread = jnp.mean(centered * centered, axis=-1, keepdims=True)
    normed = (centered * lax.rsqrt(spread + 1e-05) * gain_ref[...] + bias_ref[...]).astype(BF16)
    normed_ref[...] = normed

    projected = lax.dot_general(in_t, normed, (((1,), (1,)), ((), ())), preferred_element_type=F32)
    left = sigmoid(projected[hidden : 2 * hidden]) * projected[:hidden]
    right = sigmoid(projected[3 * hidden :]) * projected[2 * hidden : 3 * hidden]

    def by_channel(v):
        parts = [v[:, i * tokens : (i + 1) * tokens] for i in range(own)]
        return jnp.transpose(jnp.stack(parts, axis=0), (1, 0, 2)) * pair_valid

    both = jnp.concatenate([by_channel(left), by_channel(right)], axis=1)
    lr_ref[...] = both.astype(BF16)

    sends = []
    for o in range(1, peers):
        device, peer = at(o)
        sends.append(
            pltpu.make_async_remote_copy(
                src_ref=lr_ref.at[pl.ds(peer * share, share)],
                dst_ref=rx_ref.at[me],
                send_sem=a_send.at[o],
                recv_sem=a_recv.at[o],
                device_id=device,
                device_id_type=MESH,
            )
        )
    for c in sends:
        c.start()
    rx_ref[me] = lr_ref[pl.ds(me * share, share)]

    gate_ref[...] = sigmoid(
        jnp.dot(normed_ref[...], win_ref[:, 4 * hidden :], preferred_element_type=F32)
    )
    step = 128

    @pl.loop(0, own * tokens // step)
    def _(n):
        where = pl.ds(pl.multiple_of(n * step, step), step)
        part = jnp.dot(normed_ref[where], tin_ref[...], preferred_element_type=F32)
        ta, tb = part[:, :trans], part[:, trans:]
        act = (ta * sigmoid(ta) * tb).astype(BF16)
        trans_ref[where] = jnp.dot(act, tout_ref[...], preferred_element_type=F32)

    for c in sends:
        c.wait()
    mixed = []
    for h in range(share):
        block = rx_ref[:, h].astype(F32)
        lh = block[:, :own].reshape(tokens, tokens).astype(BF16)
        rh = block[:, own:].reshape(tokens, tokens).astype(BF16)
        m = lax.dot_general(lh, rh, (((1,), (1,)), ((), ())), preferred_element_type=F32)
        mixed.append(m.reshape(peers, own, tokens))
    for n in range(share // 2):
        tx_ref[:, n] = jnp.concatenate(mixed[2 * n : 2 * n + 2], axis=1).astype(BF16)
    backs = []
    for o in range(1, peers):
        device, peer = at(o)
        backs.append(
            pltpu.make_async_remote_copy(
                src_ref=tx_ref.at[peer],
                dst_ref=mx_ref.at[me],
                send_sem=b_send.at[o],
                recv_sem=b_recv.at[o],
                device_id=device,
                device_id_type=MESH,
            )
        )
    for c in backs:
        c.start()
    mx_ref[me] = tx_ref[me]
    for c in backs:
        c.wait()

    m = mx_ref[...].astype(F32).reshape(hidden, own, tokens)
    average = jnp.mean(m, axis=0, keepdims=True)
    centered = m - average
    spread = jnp.mean(centered * centered, axis=0, keepdims=True)
    scaled = jnp.transpose(centered * lax.rsqrt(spread + 1e-05), (1, 0, 2))
    for i in range(own):
        mn = (scaled[i] * fgain + fbias).T.astype(BF16)
        outgoing = jnp.dot(mn, wout_ref[...], preferred_element_type=F32)
        where = pl.ds(i * tokens, tokens)
        update_ref[i] = (gate_ref[where] * outgoing + trans_ref[where]).astype(BF16)


def fused(mesh, args):
    pair_repr, chain_ids, valid_counts = args[:3]
    norm_gain, norm_bias, input_weights, final_gain, final_bias, output_weight, tin, tout = args[3:]
    rows_n, cols_n = mesh.shape["row"], mesh.shape["col"]
    peers = rows_n * cols_n
    tokens = chain_ids.shape[0]
    own = tokens // peers
    channels = pair_repr.shape[2]
    hidden = output_weight.shape[0]
    share = hidden // peers
    vmem, anyspace = pl.BlockSpec(memory_space=pltpu.VMEM), pl.BlockSpec(memory_space=pl.ANY)
    dma = pltpu.SemaphoreType.DMA
    return pl.pallas_call(
        functools.partial(kernel, rows_n, cols_n),
        out_shape=jax.ShapeDtypeStruct((own, tokens, channels), BF16),
        in_specs=[
            anyspace,
            vmem,
            pl.BlockSpec(memory_space=pltpu.SMEM),
            vmem,
            vmem,
            anyspace,
            vmem,
            vmem,
            anyspace,
            anyspace,
            anyspace,
        ],
        out_specs=vmem,
        scratch_shapes=[
            pltpu.VMEM((own, tokens, channels), BF16),
            pltpu.VMEM(input_weights.shape, BF16),
            pltpu.VMEM(output_weight.shape, BF16),
            pltpu.VMEM(tin.shape, BF16),
            pltpu.VMEM(tout.shape, BF16),
            pltpu.VMEM((own * tokens, channels), BF16),
            pltpu.VMEM((hidden, 2 * own, tokens), BF16),
            pltpu.VMEM((peers, share, 2 * own, tokens), BF16),
            pltpu.VMEM((peers, share // 2, 2 * own, tokens), BF16),
            pltpu.VMEM((peers, share // 2, 2 * own, tokens), BF16),
            pltpu.VMEM((own * tokens, channels), F32),
            pltpu.VMEM((own * tokens, channels), F32),
            dma((5,)),
            dma((cols_n,)),
            dma((cols_n,)),
            dma((peers,)),
            dma((peers,)),
            dma((peers,)),
            dma((peers,)),
        ],
        compiler_params=pltpu.CompilerParams(
            collective_id=0, has_side_effects=True, vmem_limit_bytes=40 * 1024 * 1024
        ),
        cost_estimate=pl.CostEstimate(
            flops=10**9, bytes_accessed=4 * 10**6, transcendentals=10**6
        ),
    )(
        pair_repr,
        chain_ids.reshape(1, -1),
        valid_counts,
        norm_gain.reshape(1, -1),
        norm_bias.reshape(1, -1),
        input_weights,
        final_gain.reshape(1, -1),
        final_bias.reshape(1, -1),
        output_weight,
        tin,
        tout,
    )


def fits(mesh, args):
    peers = mesh.shape["row"] * mesh.shape["col"]
    tokens, hidden = args[1].shape[0], args[8].shape[0]
    return (
        tokens == 8 * peers
        and tokens % 128 == 0
        and tokens * tokens <= 128 * 128
        and hidden % (2 * peers) == 0
        and args[0].shape[1] % 16 == 0
        and args[0].shape[2] == 128
    )


def token_valid_of(chain_ids, valid_counts):
    token_count = chain_ids.shape[0]
    labels = jnp.arange(valid_counts.shape[0], dtype=jnp.int32)
    before = (chain_ids[:, None] < labels[None, :]).astype(jnp.int32)
    starts = jnp.sum(before, axis=0)
    member = (chain_ids[:, None] == labels[None, :]).astype(jnp.int32)
    first_index = jnp.sum(member * starts[None, :], axis=1)
    limits = jnp.sum(member * valid_counts[None, :], axis=1)
    position = jnp.arange(token_count, dtype=jnp.int32) - first_index
    return (position < limits).astype(jnp.float32)


def layer_norm(values, gain, bias):
    average = jnp.mean(values, axis=-1, keepdims=True)
    centered = values - average
    spread = jnp.mean(centered * centered, axis=-1, keepdims=True)
    return centered * lax.rsqrt(spread + 1e-05) * gain + bias


def local(
    pair_repr,
    chain_ids,
    valid_counts,
    norm_gain,
    norm_bias,
    input_weights,
    final_gain,
    final_bias,
    output_weight,
    transition_in,
    transition_out,
):
    row_count, col_count, channels = pair_repr.shape
    hidden = output_weight.shape[0]
    trans_width = transition_out.shape[0]
    token_valid = token_valid_of(chain_ids, valid_counts)
    row_start = lax.axis_index("row") * row_count
    col_start = lax.axis_index("col") * col_count
    valid_rows = lax.dynamic_slice_in_dim(token_valid, row_start, row_count)
    valid_cols = lax.dynamic_slice_in_dim(token_valid, col_start, col_count)
    pair_valid = valid_rows[:, None] * valid_cols[None, :]
    normed = layer_norm(pair_repr.astype(jnp.float32), norm_gain, norm_bias).astype(jnp.bfloat16)
    normed_flat = normed.reshape(row_count * col_count, channels)
    projected = jnp.dot(normed_flat, input_weights, preferred_element_type=jnp.float32)
    projected = projected.reshape(row_count, col_count, 4 * hidden + channels)
    left_side = (
        jax.nn.sigmoid(projected[..., hidden : 2 * hidden])
        * projected[..., :hidden]
        * pair_valid[..., None]
    ).astype(jnp.bfloat16)
    right_side = (
        jax.nn.sigmoid(projected[..., 3 * hidden : 4 * hidden])
        * projected[..., 2 * hidden : 3 * hidden]
        * pair_valid[..., None]
    ).astype(jnp.bfloat16)
    gate_value = jax.nn.sigmoid(projected[..., 4 * hidden :])
    both_parts = jnp.dot(normed_flat, transition_in, preferred_element_type=jnp.float32)
    hidden_act = (jax.nn.silu(both_parts[:, :trans_width]) * both_parts[:, trans_width:]).astype(
        jnp.bfloat16
    )
    transition = jnp.dot(hidden_act, transition_out, preferred_element_type=jnp.float32).reshape(
        row_count, col_count, channels
    )
    partials = jnp.einsum(
        "ikc,jkc->ijc",
        left_side,
        lax.all_gather(right_side, "row", axis=0, tiled=True),
        preferred_element_type=jnp.float32,
    )
    mixed_sum = lax.psum_scatter(partials, "col", scatter_dimension=1, tiled=True)
    mixed_normed = layer_norm(mixed_sum, final_gain, final_bias).astype(jnp.bfloat16)
    outgoing = jnp.dot(
        mixed_normed.reshape(row_count * col_count, hidden),
        output_weight,
        preferred_element_type=jnp.float32,
    )
    update_tile = (
        gate_value * outgoing.reshape(row_count, col_count, channels) + transition
    ).astype(jnp.bfloat16)
    return lax.all_to_all(update_tile, "col", split_axis=0, concat_axis=1, tiled=True)


def solution(mesh):
    in_specs = (
        P(("group", "row"), "col", None),
        P("group"),
        P("group"),
        P(),
        P(),
        P(),
        P(),
        P(),
        P(),
        P(),
        P(),
    )
    out_specs = P(("group", "row", "col"), None, None)

    def part(*args):
        return fused(mesh, args) if fits(mesh, args) else local(*args)

    return jax.shard_map(part, mesh=mesh, in_specs=in_specs, out_specs=out_specs, check_vma=False)
```

```python
import functools

import jax
import jax.numpy as jnp
from jax import lax
from jax.experimental import pallas as pl
from jax.experimental.pallas import tpu as pltpu
from jax.sharding import PartitionSpec as P

MESH = pl.DeviceIdType.MESH
F32, BF16 = jnp.float32, jnp.bfloat16


def sigmoid(v):
    return 0.5 * jnp.tanh(0.5 * v) + 0.5


def column_of(row):
    n = row.shape[1]
    spot = lax.broadcasted_iota(jnp.int32, (n, n), 0) == lax.broadcasted_iota(jnp.int32, (n, n), 1)
    return jnp.sum(jnp.where(spot, row, 0.0), axis=1, keepdims=True)


def kernel(
    rows_n,
    cols_n,
    pair_ref,
    ids_hbm,
    counts_hbm,
    gain_hbm,
    bias_hbm,
    in_hbm,
    fgain_hbm,
    fbias_hbm,
    out_hbm,
    tin_hbm,
    tout_hbm,
    update_ref,
    x_ref,
    ids_ref,
    counts_ref,
    gain_ref,
    bias_ref,
    fgain_ref,
    fbias_ref,
    win_ref,
    wout_ref,
    tin_ref,
    tout_ref,
    normed_ref,
    lr_ref,
    rx_ref,
    tx_ref,
    mx_ref,
    gate_ref,
    trans_ref,
    local_sem,
    in_send,
    in_recv,
    a_send,
    a_recv,
    b_send,
    b_recv,
):
    peers = rows_n * cols_n
    own, tokens, channels = x_ref.shape
    width = pair_ref.shape[1]
    hidden = wout_ref.shape[0]
    trans = tout_ref.shape[0]
    share = hidden // peers
    row, col = lax.axis_index("row"), lax.axis_index("col")
    me = row * cols_n + col

    def at(offset):
        peer = lax.rem(me + offset, peers)
        return {"row": lax.div(peer, cols_n), "col": lax.rem(peer, cols_n)}, peer

    barrier = pltpu.get_barrier_semaphore()
    for o in range(1, peers):
        pl.semaphore_signal(barrier, inc=1, device_id=at(o)[0], device_id_type=MESH)
    locals_ = [
        pltpu.make_async_copy(
            pair_ref.at[pl.ds(col * own, own)],
            x_ref.at[:, pl.ds(col * width, width), :],
            local_sem.at[0],
        )
    ]
    for n, (a, b) in enumerate(
        (
            (ids_hbm, ids_ref),
            (counts_hbm, counts_ref),
            (gain_hbm, gain_ref),
            (bias_hbm, bias_ref),
            (fgain_hbm, fgain_ref),
            (fbias_hbm, fbias_ref),
            (in_hbm, win_ref),
            (out_hbm, wout_ref),
            (tin_hbm, tin_ref),
            (tout_hbm, tout_ref),
        )
    ):
        locals_.append(pltpu.make_async_copy(a, b, local_sem.at[n + 1]))
    for c in locals_:
        c.start()
    pl.semaphore_wait(barrier, peers - 1)

    copies = []
    for o in range(1, cols_n):
        to = lax.rem(col + o, cols_n)
        copies.append(
            pltpu.make_async_remote_copy(
                src_ref=pair_ref.at[pl.ds(to * own, own)],
                dst_ref=x_ref.at[:, pl.ds(col * width, width), :],
                send_sem=in_send.at[o],
                recv_sem=in_recv.at[o],
                device_id={"row": row, "col": to},
                device_id_type=MESH,
            )
        )
    for c in copies:
        c.start()

    for c in locals_:
        c.wait()
    counts = counts_ref[...]
    ids = ids_ref[...]
    first = jnp.zeros(ids.shape, F32)
    limit = jnp.zeros(ids.shape, jnp.int32)
    for label in range(counts.shape[1]):
        start = jnp.sum(jnp.where(ids < label, 1.0, 0.0), axis=1, keepdims=True)
        first = jnp.where(ids == label, start, first)
        limit = jnp.where(ids == label, counts[:, label : label + 1], limit)
    spot = lax.broadcasted_iota(jnp.int32, ids.shape, 1).astype(F32)
    valid = jnp.where(spot - first < limit.astype(F32), 1.0, 0.0)
    wide = (own, tokens)
    mine = lax.broadcasted_iota(jnp.int32, wide, 1) == (
        me * own + lax.broadcasted_iota(jnp.int32, wide, 0)
    )
    valid_rows = jnp.sum(jnp.where(mine, valid, 0.0), axis=1, keepdims=True)
    pair_valid = valid_rows * valid
    fgain, fbias = column_of(fgain_ref[...]), column_of(fbias_ref[...])
    in_t = win_ref[:, : 4 * hidden].astype(F32).T.astype(BF16)
    for c in copies:
        c.wait()

    x = x_ref[...].reshape(own * tokens, channels).astype(F32)
    average = jnp.mean(x, axis=-1, keepdims=True)
    centered = x - average
    spread = jnp.mean(centered * centered, axis=-1, keepdims=True)
    normed = (centered * lax.rsqrt(spread + 1e-05) * gain_ref[...] + bias_ref[...]).astype(BF16)
    normed_ref[...] = normed

    projected = lax.dot_general(in_t, normed, (((1,), (1,)), ((), ())), preferred_element_type=F32)
    left = sigmoid(projected[hidden : 2 * hidden]) * projected[:hidden]
    right = sigmoid(projected[3 * hidden :]) * projected[2 * hidden : 3 * hidden]

    def by_channel(v):
        parts = [v[:, i * tokens : (i + 1) * tokens] for i in range(own)]
        return jnp.transpose(jnp.stack(parts, axis=0), (1, 0, 2)) * pair_valid

    both = jnp.concatenate([by_channel(left), by_channel(right)], axis=1)
    lr_ref[...] = both.astype(BF16)

    sends = []
    for o in range(1, peers):
        device, peer = at(o)
        sends.append(
            pltpu.make_async_remote_copy(
                src_ref=lr_ref.at[pl.ds(peer * share, share)],
                dst_ref=rx_ref.at[me],
                send_sem=a_send.at[o],
                recv_sem=a_recv.at[o],
                device_id=device,
                device_id_type=MESH,
            )
        )
    for c in sends:
        c.start()
    rx_ref[me] = lr_ref[pl.ds(me * share, share)]

    gate_ref[...] = sigmoid(
        jnp.dot(normed_ref[...], win_ref[:, 4 * hidden :], preferred_element_type=F32)
    )
    step = 128

    @pl.loop(0, own * tokens // step)
    def _(n):
        where = pl.ds(pl.multiple_of(n * step, step), step)
        part = jnp.dot(normed_ref[where], tin_ref[...], preferred_element_type=F32)
        ta, tb = part[:, :trans], part[:, trans:]
        act = (ta * sigmoid(ta) * tb).astype(BF16)
        trans_ref[where] = jnp.dot(act, tout_ref[...], preferred_element_type=F32)

    for c in sends:
        c.wait()
    mixed = []
    for h in range(share):
        block = rx_ref[:, h].astype(F32)
        lh = block[:, :own].reshape(tokens, tokens).astype(BF16)
        rh = block[:, own:].reshape(tokens, tokens).astype(BF16)
        m = lax.dot_general(lh, rh, (((1,), (1,)), ((), ())), preferred_element_type=F32)
        mixed.append(m.reshape(peers, own, tokens))
    for n in range(share // 2):
        tx_ref[:, n] = jnp.concatenate(mixed[2 * n : 2 * n + 2], axis=1).astype(BF16)
    backs = []
    for o in range(1, peers):
        device, peer = at(o)
        backs.append(
            pltpu.make_async_remote_copy(
                src_ref=tx_ref.at[peer],
                dst_ref=mx_ref.at[me],
                send_sem=b_send.at[o],
                recv_sem=b_recv.at[o],
                device_id=device,
                device_id_type=MESH,
            )
        )
    for c in backs:
        c.start()
    mx_ref[me] = tx_ref[me]
    for c in backs:
        c.wait()

    m = mx_ref[...].astype(F32).reshape(hidden, own, tokens)
    average = jnp.mean(m, axis=0, keepdims=True)
    centered = m - average
    spread = jnp.mean(centered * centered, axis=0, keepdims=True)
    scaled = jnp.transpose(centered * lax.rsqrt(spread + 1e-05), (1, 0, 2))
    for i in range(own):
        mn = (scaled[i] * fgain + fbias).T.astype(BF16)
        outgoing = jnp.dot(mn, wout_ref[...], preferred_element_type=F32)
        where = pl.ds(i * tokens, tokens)
        update_ref[i] = (gate_ref[where] * outgoing + trans_ref[where]).astype(BF16)


def fused(mesh, args):
    pair_repr, chain_ids, valid_counts = args[:3]
    norm_gain, norm_bias, input_weights, final_gain, final_bias, output_weight, tin, tout = args[3:]
    rows_n, cols_n = mesh.shape["row"], mesh.shape["col"]
    peers = rows_n * cols_n
    tokens = chain_ids.shape[0]
    own = tokens // peers
    channels = pair_repr.shape[2]
    hidden = output_weight.shape[0]
    share = hidden // peers
    vmem, hbm = pl.BlockSpec(memory_space=pltpu.VMEM), pl.BlockSpec(memory_space=pltpu.HBM)
    dma = pltpu.SemaphoreType.DMA
    return pl.pallas_call(
        functools.partial(kernel, rows_n, cols_n),
        out_shape=jax.ShapeDtypeStruct((own, tokens, channels), BF16),
        in_specs=[hbm] * 11,
        out_specs=vmem,
        scratch_shapes=[
            pltpu.VMEM((own, tokens, channels), BF16),
            pltpu.VMEM((1, tokens), jnp.int32),
            pltpu.VMEM((1, valid_counts.shape[0]), jnp.int32),
            pltpu.VMEM((1, channels), F32),
            pltpu.VMEM((1, channels), F32),
            pltpu.VMEM((1, hidden), F32),
            pltpu.VMEM((1, hidden), F32),
            pltpu.VMEM(input_weights.shape, BF16),
            pltpu.VMEM(output_weight.shape, BF16),
            pltpu.VMEM(tin.shape, BF16),
            pltpu.VMEM(tout.shape, BF16),
            pltpu.VMEM((own * tokens, channels), BF16),
            pltpu.VMEM((hidden, 2 * own, tokens), BF16),
            pltpu.VMEM((peers, share, 2 * own, tokens), BF16),
            pltpu.VMEM((peers, share // 2, 2 * own, tokens), BF16),
            pltpu.VMEM((peers, share // 2, 2 * own, tokens), BF16),
            pltpu.VMEM((own * tokens, channels), F32),
            pltpu.VMEM((own * tokens, channels), F32),
            dma((11,)),
            dma((cols_n,)),
            dma((cols_n,)),
            dma((peers,)),
            dma((peers,)),
            dma((peers,)),
            dma((peers,)),
        ],
        compiler_params=pltpu.CompilerParams(
            collective_id=0, has_side_effects=True, vmem_limit_bytes=65000000
        ),
        cost_estimate=pl.CostEstimate(
            flops=10**9, bytes_accessed=4 * 10**6, transcendentals=10**6
        ),
    )(
        pair_repr,
        chain_ids.reshape(1, -1),
        valid_counts.reshape(1, -1),
        norm_gain.reshape(1, -1),
        norm_bias.reshape(1, -1),
        input_weights,
        final_gain.reshape(1, -1),
        final_bias.reshape(1, -1),
        output_weight,
        tin,
        tout,
    )


def fits(mesh, args):
    peers = mesh.shape["row"] * mesh.shape["col"]
    tokens, hidden = args[1].shape[0], args[8].shape[0]
    return (
        tokens == 8 * peers
        and tokens % 128 == 0
        and tokens * tokens <= 128 * 128
        and hidden % (2 * peers) == 0
        and args[0].shape[1] % 16 == 0
        and args[0].shape[2] == 128
    )


def token_valid_of(chain_ids, valid_counts):
    token_count = chain_ids.shape[0]
    labels = jnp.arange(valid_counts.shape[0], dtype=jnp.int32)
    before = (chain_ids[:, None] < labels[None, :]).astype(jnp.int32)
    starts = jnp.sum(before, axis=0)
    member = (chain_ids[:, None] == labels[None, :]).astype(jnp.int32)
    first_index = jnp.sum(member * starts[None, :], axis=1)
    limits = jnp.sum(member * valid_counts[None, :], axis=1)
    position = jnp.arange(token_count, dtype=jnp.int32) - first_index
    return (position < limits).astype(jnp.float32)


def layer_norm(values, gain, bias):
    average = jnp.mean(values, axis=-1, keepdims=True)
    centered = values - average
    spread = jnp.mean(centered * centered, axis=-1, keepdims=True)
    return centered * lax.rsqrt(spread + 1e-05) * gain + bias


def local(
    pair_repr,
    chain_ids,
    valid_counts,
    norm_gain,
    norm_bias,
    input_weights,
    final_gain,
    final_bias,
    output_weight,
    transition_in,
    transition_out,
):
    row_count, col_count, channels = pair_repr.shape
    hidden = output_weight.shape[0]
    trans_width = transition_out.shape[0]
    token_valid = token_valid_of(chain_ids, valid_counts)
    row_start = lax.axis_index("row") * row_count
    col_start = lax.axis_index("col") * col_count
    valid_rows = lax.dynamic_slice_in_dim(token_valid, row_start, row_count)
    valid_cols = lax.dynamic_slice_in_dim(token_valid, col_start, col_count)
    pair_valid = valid_rows[:, None] * valid_cols[None, :]
    normed = layer_norm(pair_repr.astype(jnp.float32), norm_gain, norm_bias).astype(jnp.bfloat16)
    normed_flat = normed.reshape(row_count * col_count, channels)
    projected = jnp.dot(normed_flat, input_weights, preferred_element_type=jnp.float32)
    projected = projected.reshape(row_count, col_count, 4 * hidden + channels)
    left_side = (
        jax.nn.sigmoid(projected[..., hidden : 2 * hidden])
        * projected[..., :hidden]
        * pair_valid[..., None]
    ).astype(jnp.bfloat16)
    right_side = (
        jax.nn.sigmoid(projected[..., 3 * hidden : 4 * hidden])
        * projected[..., 2 * hidden : 3 * hidden]
        * pair_valid[..., None]
    ).astype(jnp.bfloat16)
    gate_value = jax.nn.sigmoid(projected[..., 4 * hidden :])
    both_parts = jnp.dot(normed_flat, transition_in, preferred_element_type=jnp.float32)
    hidden_act = (jax.nn.silu(both_parts[:, :trans_width]) * both_parts[:, trans_width:]).astype(
        jnp.bfloat16
    )
    transition = jnp.dot(hidden_act, transition_out, preferred_element_type=jnp.float32).reshape(
        row_count, col_count, channels
    )
    partials = jnp.einsum(
        "ikc,jkc->ijc",
        left_side,
        lax.all_gather(right_side, "row", axis=0, tiled=True),
        preferred_element_type=jnp.float32,
    )
    mixed_sum = lax.psum_scatter(partials, "col", scatter_dimension=1, tiled=True)
    mixed_normed = layer_norm(mixed_sum, final_gain, final_bias).astype(jnp.bfloat16)
    outgoing = jnp.dot(
        mixed_normed.reshape(row_count * col_count, hidden),
        output_weight,
        preferred_element_type=jnp.float32,
    )
    update_tile = (
        gate_value * outgoing.reshape(row_count, col_count, channels) + transition
    ).astype(jnp.bfloat16)
    return lax.all_to_all(update_tile, "col", split_axis=0, concat_axis=1, tiled=True)


def solution(mesh):
    in_specs = (
        P(("group", "row"), "col", None),
        P("group"),
        P("group"),
        P(),
        P(),
        P(),
        P(),
        P(),
        P(),
        P(),
        P(),
    )
    out_specs = P(("group", "row", "col"), None, None)

    def part(*args):
        return fused(mesh, args) if fits(mesh, args) else local(*args)

    return jax.shard_map(part, mesh=mesh, in_specs=in_specs, out_specs=out_specs, check_vma=False)
```

```python
import functools

import jax
import jax.numpy as jnp
from jax import lax
from jax.experimental import pallas as pl
from jax.experimental.pallas import tpu as pltpu
from jax.sharding import PartitionSpec as P

MESH = pl.DeviceIdType.MESH
F32, BF16 = jnp.float32, jnp.bfloat16


def sigmoid(v):
    return 0.5 * jnp.tanh(0.5 * v) + 0.5


def column_of(row):
    n = row.shape[1]
    spot = lax.broadcasted_iota(jnp.int32, (n, n), 0) == lax.broadcasted_iota(jnp.int32, (n, n), 1)
    return jnp.sum(jnp.where(spot, row, 0.0), axis=1, keepdims=True)


def kernel(
    rows_n,
    cols_n,
    pair_ref,
    ids_hbm,
    counts_hbm,
    gain_hbm,
    bias_hbm,
    in_hbm,
    fgain_hbm,
    fbias_hbm,
    out_hbm,
    tin_hbm,
    tout_hbm,
    update_ref,
    x_ref,
    block_ref,
    ids_ref,
    counts_ref,
    gain_ref,
    bias_ref,
    fgain_ref,
    fbias_ref,
    win_ref,
    wout_ref,
    tin_ref,
    tout_ref,
    normed_ref,
    lr_ref,
    rx_ref,
    tx_ref,
    mx_ref,
    gate_ref,
    trans_ref,
    local_sem,
    in_send,
    in_recv,
    a_send,
    a_recv,
    b_send,
    b_recv,
):
    peers = rows_n * cols_n
    own, tokens, channels = x_ref.shape
    width = pair_ref.shape[1]
    hidden = wout_ref.shape[0]
    trans = tout_ref.shape[0]
    share = hidden // peers
    row, col = lax.axis_index("row"), lax.axis_index("col")
    me = row * cols_n + col

    def at(offset):
        peer = lax.rem(me + offset, peers)
        return {"row": lax.div(peer, cols_n), "col": lax.rem(peer, cols_n)}, peer

    barrier = pltpu.get_barrier_semaphore()
    for o in range(1, peers):
        pl.semaphore_signal(barrier, inc=1, device_id=at(o)[0], device_id_type=MESH)
    locals_ = [
        pltpu.make_async_copy(
            pair_ref.at[pl.ds(col * own, own)],
            x_ref.at[:, pl.ds(col * width, width), :],
            local_sem.at[0],
        )
    ]
    for n, (a, b) in enumerate(
        (
            (pair_ref, block_ref),
            (ids_hbm, ids_ref),
            (counts_hbm, counts_ref),
            (gain_hbm, gain_ref),
            (bias_hbm, bias_ref),
            (fgain_hbm, fgain_ref),
            (fbias_hbm, fbias_ref),
            (in_hbm, win_ref),
            (out_hbm, wout_ref),
            (tin_hbm, tin_ref),
            (tout_hbm, tout_ref),
        )
    ):
        locals_.append(pltpu.make_async_copy(a, b, local_sem.at[n + 1]))
    for c in locals_:
        c.start()
    exchange = []
    for o in range(1, cols_n):
        to = lax.rem(col + o, cols_n)
        exchange.append(
            pltpu.make_async_remote_copy(
                src_ref=pair_ref.at[pl.ds(to * own, own)],
                dst_ref=x_ref.at[:, pl.ds(col * width, width), :],
                send_sem=in_send.at[o],
                recv_sem=in_recv.at[o],
                device_id={"row": row, "col": to},
                device_id_type=MESH,
            )
        )
    for c in locals_:
        c.wait()

    counts = counts_ref[...]
    ids = ids_ref[...]
    first = jnp.zeros(ids.shape, F32)
    limit = jnp.zeros(ids.shape, jnp.int32)
    for label in range(counts.shape[1]):
        start = jnp.sum(jnp.where(ids < label, 1.0, 0.0), axis=1, keepdims=True)
        first = jnp.where(ids == label, start, first)
        limit = jnp.where(ids == label, counts[:, label : label + 1], limit)
    spot = lax.broadcasted_iota(jnp.int32, ids.shape, 1).astype(F32)
    valid = jnp.where(spot - first < limit.astype(F32), 1.0, 0.0)
    wide, square = (own, tokens), (tokens, tokens)
    token = lax.broadcasted_iota(jnp.int32, wide, 1)
    in_row = (
        (token // (own * cols_n) == row)
        & (token % own == lax.broadcasted_iota(jnp.int32, wide, 0))
    )
    token = lax.broadcasted_iota(jnp.int32, square, 0)
    lane = lax.broadcasted_iota(jnp.int32, square, 1)
    to_row = ((token // own) % cols_n == lane // width).astype(F32).astype(BF16)
    to_token = (token == col * width + lane % width).astype(F32).astype(BF16)
    valid_rows = jnp.dot(
        jnp.where(in_row, valid, 0.0).astype(BF16), to_row, preferred_element_type=F32
    )
    valid_tokens = jnp.dot(
        jnp.broadcast_to(valid, wide).astype(BF16), to_token, preferred_element_type=F32
    )
    pair_valid = valid_rows * valid_tokens

    gain, bias = gain_ref[...], bias_ref[...]

    def norm(values):
        values = values.astype(F32)
        average = jnp.mean(values, axis=-1, keepdims=True)
        centered = values - average
        spread = jnp.mean(centered * centered, axis=-1, keepdims=True)
        return (centered * lax.rsqrt(spread + 1e-05) * gain + bias).astype(BF16)

    in_t = win_ref[:, : 4 * hidden].astype(F32).T.astype(BF16)
    block = block_ref[...].reshape(cols_n, own, width, channels)
    block = jnp.transpose(block, (1, 0, 2, 3)).reshape(own * tokens, channels)
    projected = lax.dot_general(
        in_t, norm(block), (((1,), (1,)), ((), ())), preferred_element_type=F32
    )
    left = sigmoid(projected[hidden : 2 * hidden]) * projected[:hidden]
    right = sigmoid(projected[3 * hidden :]) * projected[2 * hidden : 3 * hidden]

    def by_channel(v):
        parts = [v[:, i * tokens : (i + 1) * tokens] for i in range(own)]
        return jnp.transpose(jnp.stack(parts, axis=0), (1, 0, 2)) * pair_valid

    both = jnp.concatenate([by_channel(left), by_channel(right)], axis=1)
    lr_ref[...] = both.astype(BF16)
    fgain, fbias = column_of(fgain_ref[...]), column_of(fbias_ref[...])

    pl.semaphore_wait(barrier, peers - 1)
    groups = share // 2
    sends = []
    for g in range(groups):
        sends.append([])
        for o in range(1, peers):
            device, peer = at(o)
            copy = pltpu.make_async_remote_copy(
                src_ref=lr_ref.at[pl.ds(peer * share + 2 * g, 2)],
                dst_ref=rx_ref.at[g, me],
                send_sem=a_send.at[g, o],
                recv_sem=a_recv.at[g, o],
                device_id=device,
                device_id_type=MESH,
            )
            copy.start()
            sends[g].append(copy)
    for c in exchange:
        c.start()
    for g in range(groups):
        rx_ref[g, me] = lr_ref[pl.ds(me * share + 2 * g, 2)]

    backs = []
    for g in range(groups):
        for c in sends[g]:
            c.wait_recv()
        got = rx_ref[g].astype(F32).reshape(rows_n, cols_n, 2 * 2 * own, tokens)
        lane = lax.broadcasted_iota(jnp.int32, (1, 1, tokens), 2) // width
        full = []
        for a in range(cols_n):
            rows = got[:, a]
            for c in range(cols_n):
                if c != a:
                    moved = pltpu.roll(
                        got[:, c].reshape(-1, tokens), ((c - a) % cols_n) * width, 1
                    ).reshape(rows.shape)
                    rows = jnp.where(lane == c, moved, rows)
            full.append(rows.reshape(rows_n, 2, 2, own, tokens))
        full = jnp.stack(full, axis=1)
        mixed = []
        for h in range(2):
            lh = full[:, :, h, 0].reshape(tokens, tokens).astype(BF16)
            rh = full[:, :, h, 1].reshape(tokens, tokens).astype(BF16)
            m = lax.dot_general(lh, rh, (((1,), (1,)), ((), ())), preferred_element_type=F32)
            mixed.append(m.reshape(peers, own, tokens))
        tx_ref[g] = jnp.concatenate(mixed, axis=1).astype(BF16)
        for o in range(1, peers):
            device, peer = at(o)
            copy = pltpu.make_async_remote_copy(
                src_ref=tx_ref.at[g, peer],
                dst_ref=mx_ref.at[me, g],
                send_sem=b_send.at[g, o],
                recv_sem=b_recv.at[g, o],
                device_id=device,
                device_id_type=MESH,
            )
            copy.start()
            backs.append(copy)
        mx_ref[me, g] = tx_ref[g, me]

    for c in exchange:
        c.wait()
    normed_ref[...] = norm(x_ref[...].reshape(own * tokens, channels))
    gate_ref[...] = sigmoid(
        jnp.dot(normed_ref[...], win_ref[:, 4 * hidden :], preferred_element_type=F32)
    )
    step = 128

    @pl.loop(0, own * tokens // step)
    def _(n):
        where = pl.ds(pl.multiple_of(n * step, step), step)
        part = jnp.dot(normed_ref[where], tin_ref[...], preferred_element_type=F32)
        ta, tb = part[:, :trans], part[:, trans:]
        act = (ta * sigmoid(ta) * tb).astype(BF16)
        trans_ref[where] = jnp.dot(act, tout_ref[...], preferred_element_type=F32)

    for g in range(groups):
        for c in sends[g]:
            c.wait_send()
    for c in backs:
        c.wait()

    m = mx_ref[...].astype(F32).reshape(hidden, own, tokens)
    average = jnp.mean(m, axis=0, keepdims=True)
    centered = m - average
    spread = jnp.mean(centered * centered, axis=0, keepdims=True)
    scaled = jnp.transpose(centered * lax.rsqrt(spread + 1e-05), (1, 0, 2))
    for i in range(own):
        mn = (scaled[i] * fgain + fbias).T.astype(BF16)
        outgoing = jnp.dot(mn, wout_ref[...], preferred_element_type=F32)
        where = pl.ds(i * tokens, tokens)
        update_ref[i] = (gate_ref[where] * outgoing + trans_ref[where]).astype(BF16)


def fused(mesh, args):
    pair_repr, chain_ids, valid_counts = args[:3]
    norm_gain, norm_bias, input_weights, final_gain, final_bias, output_weight, tin, tout = args[3:]
    rows_n, cols_n = mesh.shape["row"], mesh.shape["col"]
    peers = rows_n * cols_n
    tokens = chain_ids.shape[0]
    own = tokens // peers
    channels = pair_repr.shape[2]
    hidden = output_weight.shape[0]
    share = hidden // peers
    vmem, hbm = pl.BlockSpec(memory_space=pltpu.VMEM), pl.BlockSpec(memory_space=pltpu.HBM)
    dma = pltpu.SemaphoreType.DMA
    return pl.pallas_call(
        functools.partial(kernel, rows_n, cols_n),
        out_shape=jax.ShapeDtypeStruct((own, tokens, channels), BF16),
        in_specs=[hbm] * 11,
        out_specs=vmem,
        scratch_shapes=[
            pltpu.VMEM((own, tokens, channels), BF16),
            pltpu.VMEM(pair_repr.shape, BF16),
            pltpu.VMEM((1, tokens), jnp.int32),
            pltpu.VMEM((1, valid_counts.shape[0]), jnp.int32),
            pltpu.VMEM((1, channels), F32),
            pltpu.VMEM((1, channels), F32),
            pltpu.VMEM((1, hidden), F32),
            pltpu.VMEM((1, hidden), F32),
            pltpu.VMEM(input_weights.shape, BF16),
            pltpu.VMEM(output_weight.shape, BF16),
            pltpu.VMEM(tin.shape, BF16),
            pltpu.VMEM(tout.shape, BF16),
            pltpu.VMEM((own * tokens, channels), BF16),
            pltpu.VMEM((hidden, 2 * own, tokens), BF16),
            pltpu.VMEM((share // 2, peers, 2, 2 * own, tokens), BF16),
            pltpu.VMEM((share // 2, peers, 2 * own, tokens), BF16),
            pltpu.VMEM((peers, share // 2, 2 * own, tokens), BF16),
            pltpu.VMEM((own * tokens, channels), F32),
            pltpu.VMEM((own * tokens, channels), F32),
            dma((12,)),
            dma((cols_n,)),
            dma((cols_n,)),
            dma((share // 2, peers)),
            dma((share // 2, peers)),
            dma((share // 2, peers)),
            dma((share // 2, peers)),
        ],
        compiler_params=pltpu.CompilerParams(
            collective_id=0, has_side_effects=True, vmem_limit_bytes=65000000
        ),
        cost_estimate=pl.CostEstimate(
            flops=10**9, bytes_accessed=4 * 10**6, transcendentals=10**6
        ),
    )(
        pair_repr,
        chain_ids.reshape(1, -1),
        valid_counts.reshape(1, -1),
        norm_gain.reshape(1, -1),
        norm_bias.reshape(1, -1),
        input_weights,
        final_gain.reshape(1, -1),
        final_bias.reshape(1, -1),
        output_weight,
        tin,
        tout,
    )


def fits(mesh, args):
    peers = mesh.shape["row"] * mesh.shape["col"]
    tokens, hidden = args[1].shape[0], args[8].shape[0]
    return (
        tokens == 8 * peers
        and tokens % 128 == 0
        and tokens * tokens <= 128 * 128
        and hidden % (2 * peers) == 0
        and args[0].shape == (8 * mesh.shape["col"], tokens // mesh.shape["col"], 128)
        and args[0].shape[1] % 16 == 0
    )


def token_valid_of(chain_ids, valid_counts):
    token_count = chain_ids.shape[0]
    labels = jnp.arange(valid_counts.shape[0], dtype=jnp.int32)
    before = (chain_ids[:, None] < labels[None, :]).astype(jnp.int32)
    starts = jnp.sum(before, axis=0)
    member = (chain_ids[:, None] == labels[None, :]).astype(jnp.int32)
    first_index = jnp.sum(member * starts[None, :], axis=1)
    limits = jnp.sum(member * valid_counts[None, :], axis=1)
    position = jnp.arange(token_count, dtype=jnp.int32) - first_index
    return (position < limits).astype(jnp.float32)


def layer_norm(values, gain, bias):
    average = jnp.mean(values, axis=-1, keepdims=True)
    centered = values - average
    spread = jnp.mean(centered * centered, axis=-1, keepdims=True)
    return centered * lax.rsqrt(spread + 1e-05) * gain + bias


def local(
    pair_repr,
    chain_ids,
    valid_counts,
    norm_gain,
    norm_bias,
    input_weights,
    final_gain,
    final_bias,
    output_weight,
    transition_in,
    transition_out,
):
    row_count, col_count, channels = pair_repr.shape
    hidden = output_weight.shape[0]
    trans_width = transition_out.shape[0]
    token_valid = token_valid_of(chain_ids, valid_counts)
    row_start = lax.axis_index("row") * row_count
    col_start = lax.axis_index("col") * col_count
    valid_rows = lax.dynamic_slice_in_dim(token_valid, row_start, row_count)
    valid_cols = lax.dynamic_slice_in_dim(token_valid, col_start, col_count)
    pair_valid = valid_rows[:, None] * valid_cols[None, :]
    normed = layer_norm(pair_repr.astype(jnp.float32), norm_gain, norm_bias).astype(jnp.bfloat16)
    normed_flat = normed.reshape(row_count * col_count, channels)
    projected = jnp.dot(normed_flat, input_weights, preferred_element_type=jnp.float32)
    projected = projected.reshape(row_count, col_count, 4 * hidden + channels)
    left_side = (
        jax.nn.sigmoid(projected[..., hidden : 2 * hidden])
        * projected[..., :hidden]
        * pair_valid[..., None]
    ).astype(jnp.bfloat16)
    right_side = (
        jax.nn.sigmoid(projected[..., 3 * hidden : 4 * hidden])
        * projected[..., 2 * hidden : 3 * hidden]
        * pair_valid[..., None]
    ).astype(jnp.bfloat16)
    gate_value = jax.nn.sigmoid(projected[..., 4 * hidden :])
    both_parts = jnp.dot(normed_flat, transition_in, preferred_element_type=jnp.float32)
    hidden_act = (jax.nn.silu(both_parts[:, :trans_width]) * both_parts[:, trans_width:]).astype(
        jnp.bfloat16
    )
    transition = jnp.dot(hidden_act, transition_out, preferred_element_type=jnp.float32).reshape(
        row_count, col_count, channels
    )
    partials = jnp.einsum(
        "ikc,jkc->ijc",
        left_side,
        lax.all_gather(right_side, "row", axis=0, tiled=True),
        preferred_element_type=jnp.float32,
    )
    mixed_sum = lax.psum_scatter(partials, "col", scatter_dimension=1, tiled=True)
    mixed_normed = layer_norm(mixed_sum, final_gain, final_bias).astype(jnp.bfloat16)
    outgoing = jnp.dot(
        mixed_normed.reshape(row_count * col_count, hidden),
        output_weight,
        preferred_element_type=jnp.float32,
    )
    update_tile = (
        gate_value * outgoing.reshape(row_count, col_count, channels) + transition
    ).astype(jnp.bfloat16)
    return lax.all_to_all(update_tile, "col", split_axis=0, concat_axis=1, tiled=True)


def solution(mesh):
    in_specs = (
        P(("group", "row"), "col", None),
        P("group"),
        P("group"),
        P(),
        P(),
        P(),
        P(),
        P(),
        P(),
        P(),
        P(),
    )
    out_specs = P(("group", "row", "col"), None, None)

    def part(*args):
        return fused(mesh, args) if fits(mesh, args) else local(*args)

    return jax.shard_map(part, mesh=mesh, in_specs=in_specs, out_specs=out_specs, check_vma=False)
```

```python
import functools

import jax
import jax.numpy as jnp
from jax import lax
from jax.experimental import pallas as pl
from jax.experimental.pallas import tpu as pltpu
from jax.sharding import PartitionSpec as P

MESH = pl.DeviceIdType.MESH
F32, BF16 = jnp.float32, jnp.bfloat16


def sigmoid(v):
    return 0.5 * jnp.tanh(0.5 * v) + 0.5


def column_of(row):
    n = row.shape[1]
    spot = lax.broadcasted_iota(jnp.int32, (n, n), 0) == lax.broadcasted_iota(jnp.int32, (n, n), 1)
    return jnp.sum(jnp.where(spot, row, 0.0), axis=1, keepdims=True)


def kernel(
    rows_n,
    cols_n,
    pair_ref,
    ids_hbm,
    counts_hbm,
    gain_hbm,
    bias_hbm,
    in_hbm,
    fgain_hbm,
    fbias_hbm,
    out_hbm,
    tin_hbm,
    tout_hbm,
    update_hbm,
    x_ref,
    block_ref,
    ids_ref,
    counts_ref,
    gain_ref,
    bias_ref,
    fgain_ref,
    fbias_ref,
    win_ref,
    wout_ref,
    tin_ref,
    tout_ref,
    lr_ref,
    rx_ref,
    tx_ref,
    mx_ref,
    gate_ref,
    trans_ref,
    local_sem,
    out_sem,
    in_send,
    in_recv,
    a_send,
    a_recv,
    b_send,
    b_recv,
):
    peers = rows_n * cols_n
    own, tokens, channels = x_ref.shape
    width = pair_ref.shape[1]
    hidden = wout_ref.shape[0]
    trans = tout_ref.shape[0]
    share = hidden // peers
    row, col = lax.axis_index("row"), lax.axis_index("col")
    me = row * cols_n + col

    def at(offset):
        peer = lax.rem(me + offset, peers)
        return {"row": lax.div(peer, cols_n), "col": lax.rem(peer, cols_n)}, peer

    barrier = pltpu.get_barrier_semaphore()
    for o in range(1, peers):
        pl.semaphore_signal(barrier, inc=1, device_id=at(o)[0], device_id_type=MESH)
    locals_ = [
        pltpu.make_async_copy(
            pair_ref.at[pl.ds(col * own, own)],
            x_ref.at[:, pl.ds(col * width, width), :],
            local_sem.at[0],
        )
    ]
    for n, (a, b) in enumerate(
        (
            (pair_ref, block_ref),
            (ids_hbm, ids_ref),
            (counts_hbm, counts_ref),
            (gain_hbm, gain_ref),
            (bias_hbm, bias_ref),
            (fgain_hbm, fgain_ref),
            (fbias_hbm, fbias_ref),
            (in_hbm, win_ref),
            (out_hbm, wout_ref),
            (tin_hbm, tin_ref),
            (tout_hbm, tout_ref),
        )
    ):
        locals_.append(pltpu.make_async_copy(a, b, local_sem.at[n + 1]))
    for c in locals_:
        c.start()
    partners = (col + 1 - 2 * lax.rem(col, 2), lax.rem(col + 2, 4), 3 - col)
    exchange = []
    for o in range(1, cols_n):
        to = partners[o - 1]
        exchange.append(
            pltpu.make_async_remote_copy(
                src_ref=pair_ref.at[pl.ds(to * own, own)],
                dst_ref=x_ref.at[:, pl.ds(col * width, width), :],
                send_sem=in_send.at[o],
                recv_sem=in_recv.at[o],
                device_id={"row": row, "col": to},
                device_id_type=MESH,
            )
        )
    for c in locals_:
        c.wait()

    counts = counts_ref[...]
    ids = ids_ref[...]
    first = jnp.zeros(ids.shape, F32)
    limit = jnp.zeros(ids.shape, jnp.int32)
    for label in range(counts.shape[1]):
        start = jnp.sum(jnp.where(ids < label, 1.0, 0.0), axis=1, keepdims=True)
        first = jnp.where(ids == label, start, first)
        limit = jnp.where(ids == label, counts[:, label : label + 1], limit)
    spot = lax.broadcasted_iota(jnp.int32, ids.shape, 1).astype(F32)
    valid = jnp.where(spot - first < limit.astype(F32), 1.0, 0.0)
    wide, square = (own, tokens), (tokens, tokens)
    token = lax.broadcasted_iota(jnp.int32, wide, 1)
    in_row = (
        (token // (own * cols_n) == row)
        & (token % own == lax.broadcasted_iota(jnp.int32, wide, 0))
    )
    token = lax.broadcasted_iota(jnp.int32, square, 0)
    lane = lax.broadcasted_iota(jnp.int32, square, 1)
    to_row = ((token // own) % cols_n == lane // width).astype(F32).astype(BF16)
    to_token = (token == col * width + lane % width).astype(F32).astype(BF16)
    valid_rows = jnp.dot(
        jnp.where(in_row, valid, 0.0).astype(BF16), to_row, preferred_element_type=F32
    )
    valid_tokens = jnp.dot(
        jnp.broadcast_to(valid, wide).astype(BF16), to_token, preferred_element_type=F32
    )
    pair_valid = valid_rows * valid_tokens

    gain, bias = gain_ref[...], bias_ref[...]

    def norm(values):
        values = values.astype(F32)
        average = jnp.mean(values, axis=-1, keepdims=True)
        centered = values - average
        spread = jnp.mean(centered * centered, axis=-1, keepdims=True)
        return (centered * lax.rsqrt(spread + 1e-05) * gain + bias).astype(BF16)

    in_t = win_ref[:, : 4 * hidden].astype(F32).T.astype(BF16)
    block = block_ref[...].reshape(cols_n, own, width, channels)
    block = jnp.transpose(block, (1, 0, 2, 3)).reshape(own * tokens, channels)
    projected = lax.dot_general(
        in_t, norm(block), (((1,), (1,)), ((), ())), preferred_element_type=F32
    )
    left = sigmoid(projected[hidden : 2 * hidden]) * projected[:hidden]
    right = sigmoid(projected[3 * hidden :]) * projected[2 * hidden : 3 * hidden]

    def by_channel(v):
        parts = [v[:, i * tokens : (i + 1) * tokens] for i in range(own)]
        return jnp.transpose(jnp.stack(parts, axis=0), (1, 0, 2)) * pair_valid

    both = jnp.concatenate([by_channel(left), by_channel(right)], axis=1)
    lr_ref[...] = both.astype(BF16)
    fgain, fbias = column_of(fgain_ref[...]), column_of(fbias_ref[...])

    pl.semaphore_wait(barrier, peers - 1)
    for c in exchange:
        c.start()
    groups = share // 2
    sends = []
    for g in range(groups):
        sends.append([])
        for o in range(1, peers):
            device, peer = at(o)
            copy = pltpu.make_async_remote_copy(
                src_ref=lr_ref.at[pl.ds(peer * share + 2 * g, 2)],
                dst_ref=rx_ref.at[g, me],
                send_sem=a_send.at[g, o],
                recv_sem=a_recv.at[g, o],
                device_id=device,
                device_id_type=MESH,
            )
            copy.start()
            sends[g].append(copy)
    for g in range(groups):
        rx_ref[g, me] = lr_ref[pl.ds(me * share + 2 * g, 2)]

    def own_rows(source):
        where = pl.ds(pl.multiple_of(source * width, width), width)
        flat, whole = (own * width, channels), (own, width, channels)
        normed = norm(x_ref[:, where, :].reshape(flat))
        gate = sigmoid(jnp.dot(normed, win_ref[:, 4 * hidden :], preferred_element_type=F32))
        gate_ref[:, where, :] = gate.reshape(whole)
        part = jnp.dot(normed, tin_ref[...], preferred_element_type=F32)
        ta, tb = part[:, :trans], part[:, trans:]
        act = (ta * sigmoid(ta) * tb).astype(BF16)
        out = jnp.dot(act, tout_ref[...], preferred_element_type=F32)
        trans_ref[:, where, :] = out.reshape(whole)

    def rest(offsets):
        for o in offsets:
            exchange[o - 1].wait_recv()
            own_rows(partners[o - 1])

    own_rows(col)
    rest((1,))
    backs = []
    for g in range(groups):
        if g == 1:
            rest(())
        for c in sends[g]:
            c.wait_recv()
        got = rx_ref[g].astype(F32).reshape(rows_n, cols_n, 2 * 2 * own, tokens)
        lane = lax.broadcasted_iota(jnp.int32, (1, 1, tokens), 2) // width
        full = []
        for a in range(cols_n):
            rows = got[:, a]
            for c in range(cols_n):
                if c != a:
                    moved = pltpu.roll(
                        got[:, c].reshape(-1, tokens), ((c - a) % cols_n) * width, 1
                    ).reshape(rows.shape)
                    rows = jnp.where(lane == c, moved, rows)
            full.append(rows.reshape(rows_n, 2, 2, own, tokens))
        full = jnp.stack(full, axis=1)
        mixed = []
        for h in range(2):
            lh = full[:, :, h, 0].reshape(tokens, tokens).astype(BF16)
            rh = full[:, :, h, 1].reshape(tokens, tokens).astype(BF16)
            m = lax.dot_general(lh, rh, (((1,), (1,)), ((), ())), preferred_element_type=F32)
            mixed.append(m.reshape(peers, own, tokens))
        tx_ref[g] = jnp.concatenate(mixed, axis=1).astype(BF16)
        for o in range(1, peers):
            device, peer = at(o)
            copy = pltpu.make_async_remote_copy(
                src_ref=tx_ref.at[g, peer],
                dst_ref=mx_ref.at[me, g],
                send_sem=b_send.at[g, o],
                recv_sem=b_recv.at[g, o],
                device_id=device,
                device_id_type=MESH,
            )
            copy.start()
            backs.append(copy)
        mx_ref[me, g] = tx_ref[g, me]

    rest((2, 3))
    for g in range(groups):
        for c in sends[g]:
            c.wait_send()
    for c in exchange:
        c.wait_send()
    for c in backs:
        c.wait()

    m = mx_ref[...].astype(F32).reshape(hidden, own, tokens)
    average = jnp.mean(m, axis=0, keepdims=True)
    centered = m - average
    spread = jnp.mean(centered * centered, axis=0, keepdims=True)
    scaled = jnp.transpose(centered * lax.rsqrt(spread + 1e-05), (1, 0, 2))
    outs = []
    for i in range(own):
        mn = (scaled[i] * fgain + fbias).T.astype(BF16)
        outgoing = jnp.dot(mn, wout_ref[...], preferred_element_type=F32)
        x_ref[i] = (gate_ref[i] * outgoing + trans_ref[i]).astype(BF16)
        out = pltpu.make_async_copy(x_ref.at[i], update_hbm.at[i], out_sem.at[i])
        out.start()
        outs.append(out)
    for c in outs:
        c.wait()


def fused(mesh, args):
    pair_repr, chain_ids, valid_counts = args[:3]
    norm_gain, norm_bias, input_weights, final_gain, final_bias, output_weight, tin, tout = args[3:]
    rows_n, cols_n = mesh.shape["row"], mesh.shape["col"]
    peers = rows_n * cols_n
    tokens = chain_ids.shape[0]
    own = tokens // peers
    channels = pair_repr.shape[2]
    hidden = output_weight.shape[0]
    share = hidden // peers
    vmem, hbm = pl.BlockSpec(memory_space=pltpu.VMEM), pl.BlockSpec(memory_space=pltpu.HBM)
    dma = pltpu.SemaphoreType.DMA
    return pl.pallas_call(
        functools.partial(kernel, rows_n, cols_n),
        out_shape=jax.ShapeDtypeStruct((own, tokens, channels), BF16),
        in_specs=[hbm] * 11,
        out_specs=hbm,
        scratch_shapes=[
            pltpu.VMEM((own, tokens, channels), BF16),
            pltpu.VMEM(pair_repr.shape, BF16),
            pltpu.VMEM((1, tokens), jnp.int32),
            pltpu.VMEM((1, valid_counts.shape[0]), jnp.int32),
            pltpu.VMEM((1, channels), F32),
            pltpu.VMEM((1, channels), F32),
            pltpu.VMEM((1, hidden), F32),
            pltpu.VMEM((1, hidden), F32),
            pltpu.VMEM(input_weights.shape, BF16),
            pltpu.VMEM(output_weight.shape, BF16),
            pltpu.VMEM(tin.shape, BF16),
            pltpu.VMEM(tout.shape, BF16),
            pltpu.VMEM((hidden, 2 * own, tokens), BF16),
            pltpu.VMEM((share // 2, peers, 2, 2 * own, tokens), BF16),
            pltpu.VMEM((share // 2, peers, 2 * own, tokens), BF16),
            pltpu.VMEM((peers, share // 2, 2 * own, tokens), BF16),
            pltpu.VMEM((own, tokens, channels), F32),
            pltpu.VMEM((own, tokens, channels), F32),
            dma((12,)),
            dma((own,)),
            dma((cols_n,)),
            dma((cols_n,)),
            dma((share // 2, peers)),
            dma((share // 2, peers)),
            dma((share // 2, peers)),
            dma((share // 2, peers)),
        ],
        compiler_params=pltpu.CompilerParams(
            collective_id=0, has_side_effects=True, vmem_limit_bytes=65000000
        ),
        cost_estimate=pl.CostEstimate(
            flops=10**9, bytes_accessed=4 * 10**6, transcendentals=10**6
        ),
    )(
        pair_repr,
        chain_ids.reshape(1, -1),
        valid_counts.reshape(1, -1),
        norm_gain.reshape(1, -1),
        norm_bias.reshape(1, -1),
        input_weights,
        final_gain.reshape(1, -1),
        final_bias.reshape(1, -1),
        output_weight,
        tin,
        tout,
    )


def fits(mesh, args):
    peers = mesh.shape["row"] * mesh.shape["col"]
    tokens, hidden = args[1].shape[0], args[8].shape[0]
    return (
        tokens == 8 * peers
        and tokens % 128 == 0
        and mesh.shape["col"] == 4
        and tokens * tokens <= 128 * 128
        and hidden % (2 * peers) == 0
        and args[0].shape == (8 * mesh.shape["col"], tokens // mesh.shape["col"], 128)
        and args[0].shape[1] % 16 == 0
    )


def token_valid_of(chain_ids, valid_counts):
    token_count = chain_ids.shape[0]
    labels = jnp.arange(valid_counts.shape[0], dtype=jnp.int32)
    before = (chain_ids[:, None] < labels[None, :]).astype(jnp.int32)
    starts = jnp.sum(before, axis=0)
    member = (chain_ids[:, None] == labels[None, :]).astype(jnp.int32)
    first_index = jnp.sum(member * starts[None, :], axis=1)
    limits = jnp.sum(member * valid_counts[None, :], axis=1)
    position = jnp.arange(token_count, dtype=jnp.int32) - first_index
    return (position < limits).astype(jnp.float32)


def layer_norm(values, gain, bias):
    average = jnp.mean(values, axis=-1, keepdims=True)
    centered = values - average
    spread = jnp.mean(centered * centered, axis=-1, keepdims=True)
    return centered * lax.rsqrt(spread + 1e-05) * gain + bias


def local(
    pair_repr,
    chain_ids,
    valid_counts,
    norm_gain,
    norm_bias,
    input_weights,
    final_gain,
    final_bias,
    output_weight,
    transition_in,
    transition_out,
):
    row_count, col_count, channels = pair_repr.shape
    hidden = output_weight.shape[0]
    trans_width = transition_out.shape[0]
    token_valid = token_valid_of(chain_ids, valid_counts)
    row_start = lax.axis_index("row") * row_count
    col_start = lax.axis_index("col") * col_count
    valid_rows = lax.dynamic_slice_in_dim(token_valid, row_start, row_count)
    valid_cols = lax.dynamic_slice_in_dim(token_valid, col_start, col_count)
    pair_valid = valid_rows[:, None] * valid_cols[None, :]
    normed = layer_norm(pair_repr.astype(jnp.float32), norm_gain, norm_bias).astype(jnp.bfloat16)
    normed_flat = normed.reshape(row_count * col_count, channels)
    projected = jnp.dot(normed_flat, input_weights, preferred_element_type=jnp.float32)
    projected = projected.reshape(row_count, col_count, 4 * hidden + channels)
    left_side = (
        jax.nn.sigmoid(projected[..., hidden : 2 * hidden])
        * projected[..., :hidden]
        * pair_valid[..., None]
    ).astype(jnp.bfloat16)
    right_side = (
        jax.nn.sigmoid(projected[..., 3 * hidden : 4 * hidden])
        * projected[..., 2 * hidden : 3 * hidden]
        * pair_valid[..., None]
    ).astype(jnp.bfloat16)
    gate_value = jax.nn.sigmoid(projected[..., 4 * hidden :])
    both_parts = jnp.dot(normed_flat, transition_in, preferred_element_type=jnp.float32)
    hidden_act = (jax.nn.silu(both_parts[:, :trans_width]) * both_parts[:, trans_width:]).astype(
        jnp.bfloat16
    )
    transition = jnp.dot(hidden_act, transition_out, preferred_element_type=jnp.float32).reshape(
        row_count, col_count, channels
    )
    partials = jnp.einsum(
        "ikc,jkc->ijc",
        left_side,
        lax.all_gather(right_side, "row", axis=0, tiled=True),
        preferred_element_type=jnp.float32,
    )
    mixed_sum = lax.psum_scatter(partials, "col", scatter_dimension=1, tiled=True)
    mixed_normed = layer_norm(mixed_sum, final_gain, final_bias).astype(jnp.bfloat16)
    outgoing = jnp.dot(
        mixed_normed.reshape(row_count * col_count, hidden),
        output_weight,
        preferred_element_type=jnp.float32,
    )
    update_tile = (
        gate_value * outgoing.reshape(row_count, col_count, channels) + transition
    ).astype(jnp.bfloat16)
    return lax.all_to_all(update_tile, "col", split_axis=0, concat_axis=1, tiled=True)


def solution(mesh):
    in_specs = (
        P(("group", "row"), "col", None),
        P("group"),
        P("group"),
        P(),
        P(),
        P(),
        P(),
        P(),
        P(),
        P(),
        P(),
    )
    out_specs = P(("group", "row", "col"), None, None)

    def part(*args):
        return fused(mesh, args) if fits(mesh, args) else local(*args)

    return jax.shard_map(part, mesh=mesh, in_specs=in_specs, out_specs=out_specs, check_vma=False)
```
